32 devices in a mesh: dp: 8 (over z, x), ctx: 4 (over y, core).
Axes of the slice: x: 2, y: 2, z: 4, core: 2. Of those that a mesh axis runs over, the one named last changes fastest.
Arguments:
- inputs: bfloat16 [8192, 768], P(('dp', 'ctx')), may hold values from -8 to 8
- cotangent: bfloat16 [8192, 768], P(('dp', 'ctx')), may hold values from -6 to 6
- norm_gain: bfloat16 [2, 768], P(None, ('dp', 'ctx')), may hold values from 0.5 to 1.5
- proj_weight: bfloat16 [2, 768, 3328], P(None, ('dp', 'ctx')), may hold values from -0.21875 to 0.21875
- step_weight: bfloat16 [2, 768, 24], P(None, ('dp', 'ctx')), may hold values from -0.21875 to 0.21875
- conv_weight: bfloat16 [2, 4, 1792], P(None, None, ('dp', 'ctx')), may hold values from -3 to 3
- conv_bias: bfloat16 [2, 1792], P(None, ('dp', 'ctx')), may hold values from -1.5 to 1.5
- gate_gain: bfloat16 [2, 1536], P(None, ('dp', 'ctx')), may hold values from 0.5 to 1.5
- out_weight: bfloat16 [2, 1536, 768], P(None, ('dp', 'ctx')), may hold values from -0.15625 to 0.15625
- step_bias: float32 [2, 24], replicated, may hold values from -4 to -1
- decay_log: float32 [2, 24], replicated, may hold values from -4 to 0.5
- skip_scale: float32 [2, 24], replicated, may hold values from 0.5 to 1.5
Outputs:
- outputs: bfloat16 [8192, 768], P(('dp', 'ctx'))
- input_grad: float32 [8192, 768], P(('dp', 'ctx'))
- norm_gain_grad: float32 [2, 768], P(None, ('dp', 'ctx'))
- proj_weight_grad: float32 [2, 768, 3328], P(None, ('dp', 'ctx'))
- step_weight_grad: float32 [2, 768, 24], P(None, ('dp', 'ctx'))
- conv_weight_grad: float32 [2, 4, 1792], P(None, None, ('dp', 'ctx'))
- conv_bias_grad: float32 [2, 1792], P(None, ('dp', 'ctx'))
- gate_gain_grad: float32 [2, 1536], P(None, ('dp', 'ctx'))
- out_weight_grad: float32 [2, 1536, 768], P(None, ('dp', 'ctx'))
- step_bias_grad: float32 [2, 24], replicated
- decay_log_grad: float32 [2, 24], replicated
- skip_scale_grad: float32 [2, 24], replicated
The draws below stay inside these ranges and needn't reach their ends.
All inputs are finite; a program needn't handle non-finite values.
Results may differ from the reference program's by a relative error of at most 0.025.
Values may be sent and summed in bfloat16 or wider, within the bound.
A program may use at most 192 MiB of HBM per device.

```python
import jax
import jax.numpy as jnp
from jax import lax

D = 768
HEADS = 24
HDIM = 64
STATE = 128
CONV = 4
GROUP = 256
LAYERS = 2
TOK_DEV = 256
INNER = 1536
TOKENS = 8192
N_DP = 8


def draw_inputs(key, part):
    key = jax.random.fold_in(key, 11)
    noise_key, piece_key = jax.random.split(key)
    noise = jnp.clip(jax.random.normal(noise_key, (TOKENS // TOK_DEV, TOK_DEV, D), jnp.float32), -5.0, 5.0)
    offset = jnp.clip(jax.random.normal(piece_key, (TOKENS // TOK_DEV, 1, D), jnp.float32), -4.0, 4.0) * 0.7
    return (noise + offset).reshape(TOKENS, D).astype(jnp.bfloat16)


def block_levels(stream_key, dims, cuts, low, high):
    def one(dim, blocks):
        steps = jax.random.uniform(jax.random.fold_in(jax.random.fold_in(stream_key, 6), dim), (blocks,), jnp.float32, low / len(cuts), high / len(cuts))
        return jnp.repeat(jnp.exp(steps), dims[dim] // blocks).reshape((-1,) + (1,) * (len(dims) - dim - 1))

    loudness = one(*cuts[0])
    for cut in cuts[1:]:
        loudness = loudness * one(*cut)
    return loudness


def bell_draw(stream_key, shape, width, limit, cuts=(), dtype=jnp.bfloat16):
    entries = jax.random.normal(stream_key, shape, jnp.float32) * width
    if len(cuts) > 0:
        entries = block_levels(stream_key, shape, cuts, -0.22, 0.18) * entries
    return jnp.clip(entries, min=-limit, max=limit).astype(dtype)


def setup_inputs(seed: int = 0) -> dict:
    arg_keys = jax.random.split(jax.random.key(seed), 13)
    return {
        "inputs": draw_inputs(jax.random.fold_in(arg_keys[12], 71), 0),
        "cotangent": bell_draw(arg_keys[1], (TOKENS, D), 1.0, 6.0, ((0, 32),)),
        "norm_gain": jnp.clip(1.0 + 0.1 * jax.random.normal(arg_keys[2], (LAYERS, D), jnp.float32), 0.5, 1.5).astype(jnp.bfloat16),
        "proj_weight": bell_draw(arg_keys[3], (LAYERS, D, 2 * INNER + 2 * STATE), D ** -0.5, 0.21875, ((1, 32),)),
        "step_weight": bell_draw(arg_keys[4], (LAYERS, D, HEADS), D ** -0.5, 0.21875, ((1, 32),)),
        "conv_weight": bell_draw(arg_keys[5], (LAYERS, CONV, INNER + 2 * STATE), CONV ** -0.5, 3.0, ((2, 32),)),
        "conv_bias": bell_draw(arg_keys[6], (LAYERS, INNER + 2 * STATE), 0.3, 1.5, ((1, 32),)),
        "gate_gain": jnp.clip(1.0 + 0.1 * jax.random.normal(arg_keys[7], (LAYERS, INNER), jnp.float32), 0.5, 1.5).astype(jnp.bfloat16),
        "out_weight": bell_draw(arg_keys[8], (LAYERS, INNER, D), INNER ** -0.5, 0.15625, ((1, 32),)),
        "step_bias": jnp.clip(jax.random.uniform(arg_keys[9], (LAYERS, HEADS), jnp.float32, -4.0, -1.0), -4.0, -1.0),
        "decay_log": jnp.clip(jax.random.uniform(arg_keys[10], (LAYERS, HEADS), jnp.float32, -4.0, 0.5), -4.0, 0.5),
        "skip_scale": jnp.clip(jax.random.uniform(arg_keys[11], (LAYERS, HEADS), jnp.float32, 0.5, 1.5), 0.5, 1.5),
    }


EPSILON = 1e-05
HIGHEST = lax.Precision.HIGHEST

@jax.custom_vjp
def low(v):
    return lax.optimization_barrier(v.astype(jnp.bfloat16)).astype(jnp.float32)

@jax.custom_vjp
def low_back(v):
    return v

def low_keep(v):
    return (low(v), None)

def low_pass(kept, grad):
    return (grad,)

def back_keep(v):
    return (v, None)

def back_low(kept, grad):
    return (low(grad),)
low.defvjp(low_keep, low_pass)
low_back.defvjp(back_keep, back_low)

def rms_scale(values, gain):
    return values * lax.rsqrt(lax.optimization_barrier(jnp.mean(values * values, axis=-1, keepdims=True)) + EPSILON) * gain

def gated_norm(values, gate_in, gain):
    return rms_scale(values * jax.nn.silu(gate_in), gain)

def conv_act(extended, kernel, offset):
    row_count = extended.shape[0] - (CONV - 1)
    summed = offset
    for tap_index in range(CONV):
        summed = summed + kernel[tap_index] * extended[tap_index:tap_index + row_count]
    return jax.nn.silu(summed)

def rates(step_raw, step_bias, decay_log):
    step_size = jax.nn.softplus(step_raw + step_bias)
    return (-step_size * jnp.exp(decay_log), step_size)

def decays(scores, decay_rate, step_size):
    cumulative = jnp.cumsum(decay_rate, axis=1)
    block_total = cumulative[:, -1]
    block_width = decay_rate.shape[1]
    causal = jnp.arange(block_width)[:, None] >= jnp.arange(block_width)[None, :]
    cum_heads = jnp.swapaxes(cumulative, 1, 2)
    difference = cum_heads[:, :, :, None] - cum_heads[:, :, None, :]
    kernel = jnp.where(causal, jnp.exp(jnp.where(causal, difference, 0.0)), 0.0)
    mixing = scores[:, None] * kernel * jnp.swapaxes(step_size, 1, 2)[:, :, None, :]
    weight = jnp.exp(block_total[:, None, :] - cumulative) * step_size
    growth = jnp.exp(cumulative)
    return (mixing, weight, growth, block_total)

def advance(state_now, inputs_pair):
    shrink_log, fresh_state = inputs_pair
    return (jnp.exp(shrink_log)[:, None, None] * state_now + fresh_state, state_now)

def mixer(hidden, norm_gain, proj_weight, step_weight, conv_weight, conv_bias, gate_gain, out_weight, step_bias, decay_log, skip_scale):
    row_count = hidden.shape[0]
    groups = row_count // GROUP
    normed = low(rms_scale(hidden, norm_gain))
    projected = low_back(jnp.dot(normed, proj_weight, precision=HIGHEST))
    step_raw = low_back(jnp.dot(normed, step_weight, precision=HIGHEST))
    gate_in = projected[:, :INNER]
    conv_in = projected[:, INNER:]
    extended = jnp.concatenate([jnp.zeros((CONV - 1, conv_in.shape[1]), jnp.float32), conv_in], 0)
    act = conv_act(extended, conv_weight, conv_bias)
    values = low(act[:, :INNER]).reshape(groups, GROUP, HEADS, HDIM)
    write_keys = low(act[:, INNER:INNER + STATE]).reshape(groups, GROUP, STATE)
    read_keys = low(act[:, INNER + STATE:]).reshape(groups, GROUP, STATE)
    decay_rate, step_size = rates(step_raw, step_bias, decay_log)
    scores = low_back(jnp.einsum('ctn,csn->cts', read_keys, write_keys, precision=HIGHEST))
    mixing, weight, growth, block_total = decays(scores, decay_rate.reshape(groups, GROUP, HEADS), step_size.reshape(groups, GROUP, HEADS))
    mixing = low(mixing)
    diagonal = jnp.einsum('chts,cshp->cthp', mixing, values, precision=HIGHEST)
    scaled = low(values * weight[..., None])
    update = low_back(jnp.einsum('cshp,csn->chpn', scaled, write_keys, precision=HIGHEST))
    _, states = lax.scan(advance, jnp.zeros((HEADS, HDIM, STATE), jnp.float32), (block_total, update))
    held = low(states)
    carried = low_back(jnp.einsum('ctn,chpn->cthp', read_keys, held, precision=HIGHEST))
    mixed_out = diagonal + growth[..., None] * carried + skip_scale[:, None] * values
    mixed_out = low_back(mixed_out.reshape(row_count, INNER))
    normed_out = low(gated_norm(mixed_out, gate_in, gate_gain))
    branch = low_back(jnp.dot(normed_out, out_weight, precision=HIGHEST))
    return hidden + branch

def network(hidden, *weights):
    for layer_index in range(LAYERS):
        hidden = mixer(hidden, *[member[layer_index] for member in weights])
    return hidden

def reference(inputs, cotangent, norm_gain, proj_weight, step_weight, conv_weight, conv_bias, gate_gain, out_weight, step_bias, decay_log, skip_scale):
    weights = (norm_gain.astype(jnp.float32), proj_weight.astype(jnp.float32), step_weight.astype(jnp.float32), conv_weight.astype(jnp.float32), conv_bias.astype(jnp.float32), gate_gain.astype(jnp.float32), out_weight.astype(jnp.float32), step_bias, decay_log, skip_scale)
    sequences = inputs.astype(jnp.float32).reshape(N_DP, -1, D)
    upstream = cotangent.astype(jnp.float32).reshape(N_DP, -1, D)

    def one_sequence(totals, inputs_pair):
        start_rows, seed_grad = inputs_pair
        result, pullback = jax.vjp(network, start_rows, *weights)
        grads = pullback(seed_grad)
        summed = tuple((first_part + second_part for first_part, second_part in zip(totals, grads[1:])))
        return (summed, (result, grads[0]))
    zeros_start = tuple((jnp.zeros_like(member) for member in weights))
    totals, (results, input_grads) = lax.scan(one_sequence, zeros_start, (sequences, upstream))
    g_norm, g_proj, g_step, g_conv, g_offset, g_gate, g_out, g_bias, g_decay, g_skip = totals
    return (results.reshape(-1, D).astype(jnp.bfloat16), input_grads.reshape(-1, D), g_norm, g_proj, g_step, g_conv, g_offset, g_gate, g_out, g_bias, g_decay, g_skip)
```

```python
import jax
import jax.numpy as jnp
from jax import lax
from jax.sharding import PartitionSpec as P

HEADS = 24
HDIM = 64
STATE = 128
CONV = 4
GROUP = 256
LAYERS = 2
INNER = 1536
CHANNELS = INNER + 2 * STATE
EXTRA = 128


EPSILON = 1e-05


def passed_along(block, axis, distance):
    devices = range(lax.axis_size(axis))
    route = [(i - distance, i) for i in devices if i - distance in devices]
    return lax.ppermute(block, axis, route)


AXES = ("dp", "ctx")


def swap_with(block, bit):
    count = lax.axis_size(AXES)
    return lax.ppermute(block, AXES, [(i, i ^ (1 << bit)) for i in range(count)])


def bit_orders():
    ctx_bits = lax.axis_size("ctx").bit_length() - 1
    all_bits = (lax.axis_size(AXES)).bit_length() - 1
    y_bits = list(range(1, ctx_bits))
    x_bits = [ctx_bits]
    z_bits = list(range(ctx_bits + 1, all_bits))
    return ([0] + y_bits + x_bits + z_bits, [0] + x_bits + z_bits + y_bits, [0] + z_bits + y_bits + x_bits)


def side(bit):
    return lax.rem(lax.div(lax.axis_index(AXES), 1 << bit), 2)


def gather_bits(shard, order):
    held, block = [], shard
    for bit in reversed(order):
        other = swap_with(block, bit)
        at = sum(1 for b in held if b > bit)
        upper = side(bit) == 1
        first = jnp.where(upper, other, block)
        second = jnp.where(upper, block, other)
        block = jnp.stack([first, second], at)
        held.append(bit)
    return block.reshape((-1,) + shard.shape)


def scatter_bits(parts, order, kind):
    bits = len(order)
    shape = parts.shape[1:]
    block = parts.reshape((2,) * bits + shape)
    held = list(range(bits - 1, -1, -1))
    for bit in order:
        at = held.index(bit)
        mine = side(bit)
        keep = lax.dynamic_index_in_dim(block, mine, at, keepdims=False)
        give = lax.dynamic_index_in_dim(block, 1 - mine, at, keepdims=False)
        got = swap_with(give, bit)
        block = keep.astype(jnp.float32) + got.astype(jnp.float32)
        held.remove(bit)
        if held:
            block = block.astype(kind)
    return block


def sum_all(block):
    for bit in range(lax.axis_size(AXES).bit_length() - 1):
        block = block + swap_with(block, bit)
    return block


def prefix(decay, state, axis, reverse):
    peers, place = (lax.axis_size(axis), lax.axis_index(axis))
    states = lax.all_gather(state.astype(jnp.bfloat16), axis)
    factors = lax.all_gather(decay.astype(jnp.bfloat16), axis).astype(jnp.float32)
    total = jnp.zeros_like(state)
    for k in range(peers):
        at = peers - 1 - k if reverse else k
        reached = at > place if reverse else at < place
        stepped = total * factors[at][:, None, None] + states[at].astype(jnp.float32)
        total = jnp.where(reached, stepped, total)
    return total


def rms_scale(values, gain):
    return values * lax.rsqrt(jnp.mean(values * values, axis=-1, keepdims=True) + EPSILON) * gain


def gated_norm(values, gate_in, gain):
    return rms_scale(values * jax.nn.silu(gate_in), gain)


def taps_sum(extended, taps, first, step, row_count):
    total = None
    for k in range(CONV):
        start = first + step * k
        term = taps[k][None, :] * extended[start : start + row_count]
        total = term if total is None else total + term
    return total


def rates(step_raw, step_bias, decay_log):
    step_size = jax.nn.softplus(step_raw + step_bias)
    return (-step_size * jnp.exp(decay_log), step_size)


def decays(scores, decay_rate, step_size):
    cumulative = jnp.cumsum(decay_rate, axis=1)
    block_total = cumulative[:, -1]
    block_width = decay_rate.shape[1]
    causal = jnp.arange(block_width)[:, None] >= jnp.arange(block_width)[None, :]
    cum_heads = jnp.swapaxes(cumulative, 1, 2)
    difference = cum_heads[:, :, :, None] - cum_heads[:, :, None, :]
    kernel = jnp.where(causal, jnp.exp(jnp.where(causal, difference, 0.0)), 0.0)
    mixing = scores[:, None] * kernel * jnp.swapaxes(step_size, 1, 2)[:, :, None, :]
    weight = jnp.exp(block_total[:, None, :] - cumulative) * step_size
    growth = jnp.exp(cumulative)
    return (mixing, weight, growth, block_total)


def advance(state_now, inputs_pair):
    shrink_log, fresh_state = inputs_pair
    return (jnp.exp(shrink_log)[:, None, None] * state_now + fresh_state, state_now)


def retreat(later_grad, inputs_pair):
    shrink_log, direct = inputs_pair
    return (direct + jnp.exp(shrink_log)[:, None, None] * later_grad, later_grad)


def contract_rows(left_side, right_side):
    return lax.dot_general(
        left_side, right_side, (((0,), (0,)), ((), ())), preferred_element_type=jnp.float32
    )


def contract_cols(left_side, right_side):
    return lax.dot_general(
        left_side, right_side, (((1,), (1,)), ((), ())), preferred_element_type=jnp.float32
    )


def forward_layer(hidden, params, head_params):
    gain_in, gate_w, conv_w, taps, offset, gain_out, out_w = params
    step_bias, decay_log, skip_scale = head_params
    row_count = hidden.shape[0]
    groups = row_count // GROUP
    scaled_in, pull_norm = jax.vjp(rms_scale, hidden, gain_in)
    normed = scaled_in.astype(jnp.bfloat16)
    conv_step = jnp.dot(normed, conv_w, preferred_element_type=jnp.float32)
    gate_in = jnp.dot(normed, gate_w, preferred_element_type=jnp.float32)
    conv_in = conv_step[:, :CHANNELS]
    step_raw = conv_step[:, CHANNELS : CHANNELS + HEADS]
    edge_rows = passed_along(conv_in[row_count - (CONV - 1) :], "ctx", 1)
    extended = jnp.concatenate([edge_rows, conv_in], 0)
    before_act = offset + taps_sum(extended, taps, 0, 1, row_count)
    act_gate = jax.nn.sigmoid(before_act)
    act = before_act * act_gate
    values = act[:, :INNER].astype(jnp.bfloat16).reshape(groups, GROUP, HEADS, HDIM)
    write_keys = act[:, INNER : INNER + STATE].astype(jnp.bfloat16).reshape(groups, GROUP, STATE)
    read_keys = act[:, INNER + STATE :].astype(jnp.bfloat16).reshape(groups, GROUP, STATE)
    (decay_rate, step_size), pull_rate = jax.vjp(rates, step_raw, step_bias, decay_log)
    scores = jnp.einsum("ctn,csn->cts", read_keys, write_keys, preferred_element_type=jnp.float32)
    (mixing, weight, growth, block_total), pull_decay = jax.vjp(
        decays,
        scores,
        decay_rate.reshape(groups, GROUP, HEADS),
        step_size.reshape(groups, GROUP, HEADS),
    )
    mixing_low = mixing.astype(jnp.bfloat16)
    diagonal = jnp.einsum("chts,cshp->cthp", mixing_low, values, preferred_element_type=jnp.float32)
    scaled = (values.astype(jnp.float32) * weight[..., None]).astype(jnp.bfloat16)
    update = jnp.einsum("cshp,csn->chpn", scaled, write_keys, preferred_element_type=jnp.float32)
    empty_state = jnp.zeros((HEADS, HDIM, STATE), jnp.float32)
    local_end, _ = lax.scan(advance, empty_state, (block_total, update))
    device_decay = jnp.exp(jnp.sum(block_total, axis=0))
    incoming = prefix(device_decay, local_end, "ctx", False)
    _, states = lax.scan(advance, incoming, (block_total, update))
    held_low = states.astype(jnp.bfloat16)
    carried = jnp.einsum("ctn,chpn->cthp", read_keys, held_low, preferred_element_type=jnp.float32)
    mixed_out = (
        diagonal + growth[..., None] * carried + skip_scale[:, None] * values.astype(jnp.float32)
    )
    mixed_out = mixed_out.reshape(row_count, INNER)
    normed_float, pull_gate = jax.vjp(gated_norm, mixed_out, gate_in, gain_out)
    normed_out = normed_float.astype(jnp.bfloat16)
    branch = jnp.dot(normed_out, out_w, preferred_element_type=jnp.float32)
    kept_values = (
        normed,
        pull_norm,
        extended,
        before_act,
        act_gate,
        pull_rate,
        pull_decay,
        values,
        write_keys,
        read_keys,
        mixing_low,
        scaled,
        states,
        held_low,
        carried,
        growth,
        weight,
        block_total,
        device_decay,
        pull_gate,
        normed_out,
    )
    return (hidden + branch, kept_values)


def backward_layer(grad_hidden, params, head_params, kept_values):
    gain_in, gate_w, conv_w, taps, offset, gain_out, out_w = params
    skip_scale = head_params[2]
    (
        normed,
        pull_norm,
        extended,
        before_act,
        act_gate,
        pull_rate,
        pull_decay,
        values,
        write_keys,
        read_keys,
        mixing_low,
        scaled,
        states,
        held_low,
        carried,
        growth,
        weight,
        block_total,
        device_decay,
        pull_gate,
        normed_out,
    ) = kept_values
    row_count = grad_hidden.shape[0]
    groups = row_count // GROUP
    grad_branch = grad_hidden.astype(jnp.bfloat16)
    out_grad = contract_rows(normed_out, grad_branch)
    grad_normed = contract_cols(grad_branch, out_w)
    grad_mixed, grad_gate, gain_out_grad = pull_gate(grad_normed)
    grad_y = grad_mixed.astype(jnp.bfloat16).reshape(groups, GROUP, HEADS, HDIM)
    grad_float = grad_y.astype(jnp.float32)
    grad_mixing = jnp.einsum("cthp,cshp->chts", grad_y, values, preferred_element_type=jnp.float32)
    grad_values = jnp.einsum(
        "chts,cthp->cshp", mixing_low, grad_y, preferred_element_type=jnp.float32
    )
    grad_values = grad_values + skip_scale[:, None] * grad_float
    skip_grad = jnp.sum(grad_float * values, axis=(0, 1, 3))
    grad_growth = jnp.sum(grad_float * carried, axis=-1)
    grad_carried = (growth[..., None] * grad_float).astype(jnp.bfloat16)
    grad_read = jnp.einsum(
        "cthp,chpn->ctn", grad_carried, held_low, preferred_element_type=jnp.float32
    )
    grad_held = jnp.einsum(
        "cthp,ctn->chpn", grad_carried, read_keys, preferred_element_type=jnp.float32
    )
    empty_state = jnp.zeros((HEADS, HDIM, STATE), jnp.float32)
    local_start, _ = lax.scan(retreat, empty_state, (block_total, grad_held), reverse=True)
    outgoing = prefix(device_decay, local_start, "ctx", True)
    _, after_grad = lax.scan(retreat, outgoing, (block_total, grad_held), reverse=True)
    grad_total = jnp.exp(block_total) * jnp.sum(after_grad * states, axis=(2, 3))
    grad_update = after_grad.astype(jnp.bfloat16)
    grad_scaled = jnp.einsum(
        "chpn,csn->cshp", grad_update, write_keys, preferred_element_type=jnp.float32
    )
    grad_write = jnp.einsum(
        "chpn,cshp->csn", grad_update, scaled, preferred_element_type=jnp.float32
    )
    grad_values = grad_values + grad_scaled * weight[..., None]
    grad_weight = jnp.sum(grad_scaled * values, axis=-1)
    grad_scores, grad_rate, grad_step = pull_decay(
        (grad_mixing, grad_weight, grad_growth, grad_total)
    )
    grad_scores_low = grad_scores.astype(jnp.bfloat16)
    grad_read = grad_read + jnp.einsum(
        "cts,csn->ctn", grad_scores_low, write_keys, preferred_element_type=jnp.float32
    )
    grad_write = grad_write + jnp.einsum(
        "cts,ctn->csn", grad_scores_low, read_keys, preferred_element_type=jnp.float32
    )
    grad_raw, bias_grad, decay_grad = pull_rate(
        (grad_rate.reshape(row_count, HEADS), grad_step.reshape(row_count, HEADS))
    )
    grad_act = jnp.concatenate(
        [
            grad_values.reshape(row_count, INNER),
            grad_write.reshape(row_count, STATE),
            grad_read.reshape(row_count, STATE),
        ],
        1,
    )
    grad_before = grad_act * (act_gate * (1.0 + before_act * (1.0 - act_gate)))
    next_rows = passed_along(grad_before[: CONV - 1], "ctx", -1)
    grad_conv_in = taps_sum(
        jnp.concatenate([grad_before, next_rows], 0), taps, CONV - 1, -1, row_count
    )
    tap_grads = [
        jnp.sum(grad_before * extended[k : k + row_count], axis=0) for k in range(CONV)
    ]
    offset_grad = jnp.sum(grad_before, axis=0)
    grad_gate_low = grad_gate.astype(jnp.bfloat16)
    grad_conv_low = jnp.concatenate(
        [grad_conv_in, jnp.pad(grad_raw, ((0, 0), (0, EXTRA - HEADS)))], 1
    ).astype(jnp.bfloat16)
    gate_w_grad = contract_rows(normed, grad_gate_low)
    conv_w_grad = contract_rows(normed, grad_conv_low)
    grad_normed_in = contract_cols(grad_gate_low, gate_w) + contract_cols(grad_conv_low, conv_w)
    grad_input, gain_in_grad = pull_norm(grad_normed_in)
    weight_grads = (gate_w_grad, conv_w_grad, out_grad)
    small_grads = (gain_in_grad, tap_grads, offset_grad, gain_out_grad)
    return (grad_hidden + grad_input, weight_grads, small_grads, (bias_grad, decay_grad, skip_grad))


def on_device(
    inputs,
    cotangent,
    norm_gain,
    proj_weight,
    step_weight,
    conv_weight,
    conv_bias,
    gate_gain,
    out_weight,
    step_bias,
    decay_log,
    skip_scale,
):
    count = lax.axis_size(AXES)
    orders = bit_orders()
    d_own, ch_own, in_own = (norm_gain.shape[1], conv_bias.shape[1], gate_gain.shape[1])
    smalls = jnp.concatenate(
        [
            norm_gain.reshape(-1),
            gate_gain.reshape(-1),
            conv_bias.reshape(-1),
            conv_weight.reshape(-1),
        ]
    )
    smalls = gather_bits(smalls, orders[0]).astype(jnp.float32)
    cut = 0
    rows = []
    for own, number in ((d_own, LAYERS), (in_own, LAYERS), (ch_own, LAYERS), (ch_own, LAYERS * CONV)):
        rows.append([smalls[:, cut + i * own : cut + (i + 1) * own].reshape(-1) for i in range(number)])
        cut += own * number
    gain_rows, gate_rows, bias_rows, tap_rows = rows

    def gather_layer(shards):
        gate_part, conv_part, out_part = shards
        return (
            gather_bits(gate_part, orders[0]).reshape(-1, INNER),
            gather_bits(conv_part, orders[1]).reshape(-1, CHANNELS + EXTRA),
            gather_bits(out_part, orders[2]).reshape(INNER, -1),
        )

    shards = []
    for layer in range(LAYERS):
        shards.append(
            (
                proj_weight[layer, :, :INNER],
                jnp.concatenate(
                    [
                        proj_weight[layer, :, INNER:],
                        jnp.pad(step_weight[layer], ((0, 0), (0, EXTRA - HEADS))),
                    ],
                    1,
                ),
                out_weight[layer],
            )
        )
    gathered = []
    for layer in range(LAYERS):
        if layer > 0:
            shards[layer], _ = lax.optimization_barrier((shards[layer], gathered[layer - 1]))
        gathered.append(gather_layer(shards[layer]))

    hidden = inputs.astype(jnp.float32)
    saved_list, params_list = ([], [])
    for layer in range(LAYERS):
        gate_w, conv_w, out_w = gathered[layer]
        params = (
            gain_rows[layer],
            gate_w,
            conv_w,
            tap_rows[layer * CONV : (layer + 1) * CONV],
            bias_rows[layer],
            gate_rows[layer],
            out_w,
        )
        params_list.append(params)
        head_params = (step_bias[layer], decay_log[layer], skip_scale[layer])
        hidden, kept_values = forward_layer(hidden, params, head_params)
        saved_list.append(kept_values)
    outputs = hidden.astype(jnp.bfloat16)
    grad_hidden = cotangent.astype(jnp.float32)
    summed = [None] * LAYERS
    small_list = [None] * LAYERS
    head_list = [None] * LAYERS
    for layer in reversed(range(LAYERS)):
        head_params = (step_bias[layer], decay_log[layer], skip_scale[layer])
        grad_hidden, weight_grads, small_grads, head_grads = backward_layer(
            grad_hidden, params_list[layer], head_params, saved_list[layer]
        )
        summed[layer] = tuple(
            scatter_bits(
                grad.astype(jnp.bfloat16).reshape(count, -1, grad.shape[1]), order, jnp.bfloat16
            )
            for grad, order in zip(weight_grads, orders)
        )
        gain_in_grad, tap_grads, offset_grad, gain_out_grad = small_grads
        small_list[layer] = jnp.concatenate(
            [row.reshape(count, -1) for row in (gain_in_grad, gain_out_grad, offset_grad, *tap_grads)], 1
        )
        head_list[layer] = jnp.stack(head_grads)
    small_sums = scatter_bits(jnp.stack(small_list, 1), orders[0], jnp.float32)
    head_sums = sum_all(jnp.stack(head_list, 1))
    edge = d_own + in_own
    proj_all = jnp.stack(
        [jnp.concatenate([gate, conv[:, :CHANNELS]], 1) for gate, conv, _ in summed]
    )
    rate_all = jnp.stack([conv[:, CHANNELS : CHANNELS + HEADS] for _, conv, _ in summed])
    out_all = jnp.stack([out for _, _, out in summed])
    return (
        outputs,
        grad_hidden,
        small_sums[:, :d_own],
        proj_all,
        rate_all,
        small_sums[:, edge + ch_own :].reshape(LAYERS, CONV, ch_own),
        small_sums[:, edge : edge + ch_own],
        small_sums[:, d_own:edge],
        out_all,
        head_sums[0],
        head_sums[1],
        head_sums[2],
    )


def solution(mesh):
    in_specs = (
        P(("dp", "ctx"), None),
        P(("dp", "ctx"), None),
        P(None, ("dp", "ctx")),
        P(None, ("dp", "ctx"), None),
        P(None, ("dp", "ctx"), None),
        P(None, None, ("dp", "ctx")),
        P(None, ("dp", "ctx")),
        P(None, ("dp", "ctx")),
        P(None, ("dp", "ctx"), None),
        P(),
        P(),
        P(),
    )
    out_specs = (
        P(("dp", "ctx"), None),
        P(("dp", "ctx"), None),
        P(None, ("dp", "ctx")),
        P(None, ("dp", "ctx"), None),
        P(None, ("dp", "ctx"), None),
        P(None, None, ("dp", "ctx")),
        P(None, ("dp", "ctx")),
        P(None, ("dp", "ctx")),
        P(None, ("dp", "ctx"), None),
        P(),
        P(),
        P(),
    )
    return jax.shard_map(
        on_device, mesh=mesh, in_specs=in_specs, out_specs=out_specs, check_vma=False
    )
```

```python
import jax
import jax.numpy as jnp
from jax import lax
from jax.experimental import pallas as pl
from jax.experimental.pallas import tpu as pltpu
from jax.sharding import PartitionSpec as P

HEADS = 24
HDIM = 64
STATE = 128
CONV = 4
GROUP = 256
LAYERS = 2
INNER = 1536
CHANNELS = INNER + 2 * STATE
EXTRA = 128


EPSILON = 1e-05


def passed_along(block, axis, distance):
    devices = range(lax.axis_size(axis))
    route = [(i - distance, i) for i in devices if i - distance in devices]
    return lax.ppermute(block, axis, route)


AXES = ("dp", "ctx")


def swap_with(block, bit):
    count = lax.axis_size(AXES)
    return lax.ppermute(block, AXES, [(i, i ^ (1 << bit)) for i in range(count)])


def bit_orders():
    ctx_bits = lax.axis_size("ctx").bit_length() - 1
    all_bits = (lax.axis_size(AXES)).bit_length() - 1
    y_bits = list(range(1, ctx_bits))
    x_bits = [ctx_bits]
    z_bits = list(range(ctx_bits + 1, all_bits))
    return ([0] + y_bits + x_bits + z_bits, [0] + x_bits + z_bits + y_bits, [0] + z_bits + y_bits + x_bits)


def side(bit):
    return lax.rem(lax.div(lax.axis_index(AXES), 1 << bit), 2)


def gather_bits(shard, order):
    held, block = [], shard
    for bit in reversed(order):
        other = swap_with(block, bit)
        at = sum(1 for b in held if b > bit)
        upper = side(bit) == 1
        first = jnp.where(upper, other, block)
        second = jnp.where(upper, block, other)
        block = jnp.stack([first, second], at)
        held.append(bit)
    return block.reshape((-1,) + shard.shape)


def scatter_bits(parts, order, kind):
    bits = len(order)
    shape = parts.shape[1:]
    block = parts.reshape((2,) * bits + shape)
    held = list(range(bits - 1, -1, -1))
    for bit in order:
        at = held.index(bit)
        mine = side(bit)
        keep = lax.dynamic_index_in_dim(block, mine, at, keepdims=False)
        give = lax.dynamic_index_in_dim(block, 1 - mine, at, keepdims=False)
        got = swap_with(give, bit)
        block = keep.astype(jnp.float32) + got.astype(jnp.float32)
        held.remove(bit)
        if held:
            block = block.astype(kind)
    return block


def sum_all(block):
    for bit in range(lax.axis_size(AXES).bit_length() - 1):
        block = block + swap_with(block, bit)
    return block


def prefix(decay, state, axis, reverse):
    peers, place = (lax.axis_size(axis), lax.axis_index(axis))
    states = lax.all_gather(state.astype(jnp.bfloat16), axis)
    factors = lax.all_gather(decay.astype(jnp.bfloat16), axis).astype(jnp.float32)
    total = jnp.zeros_like(state)
    for k in range(peers):
        at = peers - 1 - k if reverse else k
        reached = at > place if reverse else at < place
        stepped = total * factors[at][:, None, None] + states[at].astype(jnp.float32)
        total = jnp.where(reached, stepped, total)
    return total


def rms_scale(values, gain):
    return values * lax.rsqrt(jnp.mean(values * values, axis=-1, keepdims=True) + EPSILON) * gain


def gated_norm(values, gate_in, gain):
    return rms_scale(values * jax.nn.silu(gate_in), gain)


def taps_sum(extended, taps, first, step, row_count):
    total = None
    for k in range(CONV):
        start = first + step * k
        term = taps[k][None, :] * extended[start : start + row_count]
        total = term if total is None else total + term
    return total


def rates(step_raw, step_bias, decay_log):
    step_size = jax.nn.softplus(step_raw + step_bias)
    return (-step_size * jnp.exp(decay_log), step_size)


def mm(left, right, dims, exact=False):
    return lax.dot_general(
        left,
        right,
        ((dims[:1], dims[1:]), ((), ())),
        precision=lax.Precision.HIGHEST if exact else None,
        preferred_element_type=jnp.float32,
    )


PAIR = 2 * HDIM
PAIRS = HEADS // 2


def left_half(rows):
    return lax.broadcasted_iota(jnp.int32, (rows, PAIR), 1) < HDIM


def pair_of(ref, j, half):
    return jnp.where(half, ref[:, 2 * j : 2 * j + 1], ref[:, 2 * j + 1 : 2 * j + 2])


def head_sum(j):
    lane = lax.broadcasted_iota(jnp.int32, (PAIR, 128), 0)
    head = lax.broadcasted_iota(jnp.int32, (PAIR, 128), 1)
    return (head == 2 * j + jnp.where(lane < HDIM, 0, 1)).astype(jnp.float32)


def decay_kernel(cum, cum_t, h, causal):
    difference = cum[:, h : h + 1] - cum_t[h : h + 1, :]
    return jnp.exp(jnp.where(causal, difference, -jnp.inf))


def causal_mask(rows):
    return lax.broadcasted_iota(jnp.int32, (rows, rows), 0) >= lax.broadcasted_iota(
        jnp.int32, (rows, rows), 1
    )


def mix_forward(
    values, write, read, cum, cum_t, step_t, state, gate, skip, gain, normed, mixed, inverse, kept
):
    rows = values.shape[0]
    half, causal = (left_half(rows), causal_mask(rows))
    scores = mm(read[...], write[...], (1, 1))
    squares = jnp.zeros((rows, PAIR), jnp.float32)
    for j in range(PAIRS):
        at = slice(j * PAIR, (j + 1) * PAIR)
        pair = values[:, at]
        parts = []
        for h in (2 * j, 2 * j + 1):
            mixing = scores * decay_kernel(cum, cum_t, h, causal) * step_t[h : h + 1, :]
            parts.append(mm(mixing.astype(jnp.bfloat16), pair, (1, 0)))
        carried = mm(read[...], state[at, :].astype(jnp.bfloat16), (1, 1))
        out = (
            jnp.where(half, parts[0], parts[1])
            + jnp.exp(pair_of(cum, j, half)) * carried
            + skip[:, at] * pair.astype(jnp.float32)
        )
        mixed[:, at] = out
        gated = out * jax.nn.silu(gate[:, at])
        kept[:, at] = gated
        squares += gated * gated
    scale = lax.rsqrt(jnp.sum(squares, axis=1, keepdims=True) / INNER + EPSILON)
    inverse[...] = jnp.broadcast_to(scale, (rows, PAIR))
    for j in range(PAIRS):
        at = slice(j * PAIR, (j + 1) * PAIR)
        normed[:, at] = (kept[:, at] * scale * gain[:, at]).astype(jnp.bfloat16)


def gate_backward(
    grad, values, read, cum, state, gate, gain, mixed, inverse,
    grad_y, grad_gate, gain_grad, skip_grad, growth_grad, read_grad, held_grad,
):
    rows = values.shape[0]
    half = left_half(rows)
    scale = inverse[...]
    total = jnp.zeros((rows, PAIR), jnp.float32)
    for j in range(PAIRS):
        at = slice(j * PAIR, (j + 1) * PAIR)
        unit = mixed[:, at] * jax.nn.silu(gate[:, at]) * scale
        product = grad[:, at] * unit
        gain_grad[:, at] = jnp.sum(product, axis=0, keepdims=True)
        total += product * gain[:, at]
    mean = jnp.sum(total, axis=1, keepdims=True) / INNER
    growths = jnp.zeros((rows, 128), jnp.float32)
    reads = jnp.zeros((rows, STATE), jnp.float32)
    for j in range(PAIRS):
        at = slice(j * PAIR, (j + 1) * PAIR)
        gate_now, mixed_now = (gate[:, at], mixed[:, at])
        sig = jax.nn.sigmoid(gate_now)
        silu = gate_now * sig
        direct = scale * (grad[:, at] * gain[:, at] - mixed_now * silu * scale * mean)
        low = (direct * silu).astype(jnp.bfloat16)
        grad_y[:, at] = low
        slope = sig * (1.0 + gate_now * (1.0 - sig))
        grad_gate[:, at] = (direct * mixed_now * slope).astype(jnp.bfloat16)
        wide = low.astype(jnp.float32)
        held = state[at, :].astype(jnp.bfloat16)
        carried = mm(read[...], held, (1, 1))
        growths += mm(wide * carried, head_sum(j), (1, 0), True)
        skip_grad[:, at] = jnp.sum(wide * values[:, at].astype(jnp.float32), axis=0, keepdims=True)
        grad_carried = (jnp.exp(pair_of(cum, j, half)) * wide).astype(jnp.bfloat16)
        reads += mm(grad_carried, held, (1, 0))
        held_grad[at, :] = mm(grad_carried, read[...], (0, 0))
    growth_grad[...] = growths
    read_grad[...] = reads


def mix_backward(
    grad_y, values, write, read, cum, cum_t, step_t, weight, after, skip, read_part,
    grad_values, grad_write, grad_read, row_grad, column_grad, weight_grad,
):
    rows = values.shape[0]
    half, causal = (left_half(rows), causal_mask(rows))
    scores = mm(read[...], write[...], (1, 1))
    score_grad = jnp.zeros((rows, rows), jnp.float32)
    writes = jnp.zeros((rows, STATE), jnp.float32)
    weights = jnp.zeros((rows, 128), jnp.float32)
    for j in range(PAIRS):
        at = slice(j * PAIR, (j + 1) * PAIR)
        pair, upper = (values[:, at], grad_y[:, at])
        wide, upper_wide = (pair.astype(jnp.float32), upper.astype(jnp.float32))
        update = after[at, :].astype(jnp.bfloat16)
        scaled_grad = mm(write[...], update, (1, 1))
        spread = pair_of(weight, j, half)
        writes += mm((wide * spread).astype(jnp.bfloat16), update, (1, 0))
        parts = []
        for i in range(2):
            h = 2 * j + i
            own = jnp.where(half if i == 0 else jnp.logical_not(half), upper_wide, 0.0)
            mixing_grad = mm(own.astype(jnp.bfloat16), pair, (1, 1))
            factor = decay_kernel(cum, cum_t, h, causal)
            stepped = factor * step_t[h : h + 1, :]
            mixing = scores * stepped
            score_grad += mixing_grad * stepped
            row_grad[:, h : h + 1] = jnp.sum(mixing_grad * mixing, axis=1, keepdims=True)
            column_grad[h : h + 1, :] = jnp.sum(
                mixing_grad * (scores * factor), axis=0, keepdims=True
            )
            parts.append(mm(mixing.astype(jnp.bfloat16), upper, (0, 0)))
        grad_values[:, at] = (
            jnp.where(half, parts[0], parts[1]) + skip[:, at] * upper_wide + scaled_grad * spread
        )
        weights += mm(scaled_grad * wide, head_sum(j), (1, 0), True)
    low = score_grad.astype(jnp.bfloat16)
    grad_read[...] = read_part[...] + mm(low, write[...], (1, 0))
    grad_write[...] = writes + mm(low, read[...], (0, 0))
    weight_grad[...] = weights


def on_core(body, outs, scratch=()):
    return pl.pallas_call(
        body,
        out_shape=[jax.ShapeDtypeStruct(shape, kind) for shape, kind in outs],
        scratch_shapes=list(scratch),
        compiler_params=pltpu.CompilerParams(vmem_limit_bytes=28 * 1024 * 1024),
    )


def lower_ones(rows):
    return causal_mask(rows).astype(jnp.float32)


def contract_rows(left_side, right_side):
    return lax.dot_general(
        left_side, right_side, (((0,), (0,)), ((), ())), preferred_element_type=jnp.float32
    )


def contract_cols(left_side, right_side):
    return lax.dot_general(
        left_side, right_side, (((1,), (1,)), ((), ())), preferred_element_type=jnp.float32
    )


def forward_layer(hidden, params, head_params):
    gain_in, gate_w, conv_w, taps, offset, gain_out, out_w = params
    step_bias, decay_log, skip_scale = head_params
    row_count = hidden.shape[0]
    assert row_count == GROUP
    scaled_in, pull_norm = jax.vjp(rms_scale, hidden, gain_in)
    normed = scaled_in.astype(jnp.bfloat16)
    conv_step = jnp.dot(normed, conv_w, preferred_element_type=jnp.float32)
    gate_in = jnp.dot(normed, gate_w, preferred_element_type=jnp.float32)
    conv_in = conv_step[:, :CHANNELS]
    step_raw = conv_step[:, CHANNELS : CHANNELS + HEADS]
    edge_rows = passed_along(conv_in[row_count - (CONV - 1) :], "ctx", 1)
    extended = jnp.concatenate([edge_rows, conv_in], 0)
    before_act = offset + taps_sum(extended, taps, 0, 1, row_count)
    act_gate = jax.nn.sigmoid(before_act)
    act = before_act * act_gate
    act_low = act.astype(jnp.bfloat16)
    values = act_low[:, :INNER]
    write_keys = act_low[:, INNER : INNER + STATE]
    read_keys = act_low[:, INNER + STATE :]
    (decay_rate, step_size), pull_rate = jax.vjp(rates, step_raw, step_bias, decay_log)
    cumulative = mm(lower_ones(row_count), decay_rate, (1, 0), True)
    block_total = cumulative[-1]
    shrink = jnp.exp(block_total[None, :] - cumulative)
    weight = shrink * step_size
    cum_t, step_t = (cumulative.T, step_size.T)
    spread = jnp.broadcast_to(weight[:, :, None], (row_count, HEADS, HDIM)).reshape(row_count, INNER)
    scaled = (values.astype(jnp.float32) * spread).astype(jnp.bfloat16)
    update = contract_rows(scaled, write_keys).reshape(HEADS, HDIM, STATE)
    device_decay = jnp.exp(block_total)
    incoming = prefix(device_decay, update, "ctx", False).reshape(INNER, STATE)
    skip_row = jnp.repeat(skip_scale, HDIM)[None, :]
    wide = (row_count, INNER)
    normed_out, mixed_out, inverse = on_core(
        mix_forward,
        [(wide, jnp.bfloat16), (wide, jnp.float32), ((row_count, PAIR), jnp.float32)],
        [pltpu.VMEM(wide, jnp.float32)],
    )(
        values, write_keys, read_keys, cumulative, cum_t, step_t, incoming, gate_in,
        skip_row, gain_out[None, :],
    )
    branch = jnp.dot(normed_out, out_w, preferred_element_type=jnp.float32)
    kept_values = (
        normed,
        pull_norm,
        extended,
        before_act,
        act_gate,
        pull_rate,
        values,
        write_keys,
        read_keys,
        cumulative,
        cum_t,
        step_t,
        step_size,
        shrink,
        weight,
        device_decay,
        incoming,
        skip_row,
        gate_in,
        mixed_out,
        inverse,
        normed_out,
    )
    return (hidden + branch, kept_values)


def backward_layer(grad_hidden, params, head_params, kept_values):
    gain_in, gate_w, conv_w, taps, offset, gain_out, out_w = params
    skip_scale = head_params[2]
    (
        normed,
        pull_norm,
        extended,
        before_act,
        act_gate,
        pull_rate,
        values,
        write_keys,
        read_keys,
        cumulative,
        cum_t,
        step_t,
        step_size,
        shrink,
        weight,
        device_decay,
        incoming,
        skip_row,
        gate_in,
        mixed_out,
        inverse,
        normed_out,
    ) = kept_values
    row_count = grad_hidden.shape[0]
    grad_branch = grad_hidden.astype(jnp.bfloat16)
    out_grad = contract_rows(normed_out, grad_branch)
    grad_normed = contract_cols(grad_branch, out_w)
    wide, keys = ((row_count, INNER), (row_count, STATE))
    row = (1, INNER)
    grad_y, grad_gate_low, gain_out_grad, skip_grad, growth_grad, read_part, grad_held = on_core(
        gate_backward,
        [
            (wide, jnp.bfloat16), (wide, jnp.bfloat16), (row, jnp.float32), (row, jnp.float32),
            ((row_count, 128), jnp.float32), (keys, jnp.float32), ((INNER, STATE), jnp.float32),
        ],
    )(grad_normed, values, read_keys, cumulative, incoming, gate_in, gain_out[None, :], mixed_out, inverse)
    skip_grad = jnp.sum(skip_grad.reshape(HEADS, HDIM), axis=1)
    outgoing = prefix(device_decay, grad_held.reshape(HEADS, HDIM, STATE), "ctx", True)
    grad_total = device_decay * jnp.sum(
        outgoing * incoming.reshape(HEADS, HDIM, STATE), axis=(1, 2)
    )
    grad_values, grad_write, grad_read, row_grad, column_grad, weight_grad = on_core(
        mix_backward,
        [
            (wide, jnp.float32), (keys, jnp.float32), (keys, jnp.float32),
            ((row_count, HEADS), jnp.float32), ((HEADS, row_count), jnp.float32),
            ((row_count, 128), jnp.float32),
        ],
    )(
        grad_y, values, write_keys, read_keys, cumulative, cum_t, step_t, weight,
        outgoing.reshape(INNER, STATE), skip_row, read_part,
    )
    growth_grad, weight_grad = (growth_grad[:, :HEADS], weight_grad[:, :HEADS])
    column_grad = column_grad.T
    through_weight = weight * weight_grad
    grad_cum = (
        row_grad - step_size * column_grad + jnp.exp(cumulative) * growth_grad - through_weight
    )
    grad_total = grad_total + jnp.sum(through_weight, axis=0)
    grad_rate = mm(lower_ones(row_count), grad_cum, (0, 0), True) + grad_total
    grad_step = column_grad + shrink * weight_grad
    grad_raw, bias_grad, decay_grad = pull_rate((grad_rate, grad_step))
    grad_act = jnp.concatenate([grad_values, grad_write, grad_read], 1)
    grad_before = grad_act * (act_gate * (1.0 + before_act * (1.0 - act_gate)))
    next_rows = passed_along(grad_before[: CONV - 1], "ctx", -1)
    grad_conv_in = taps_sum(
        jnp.concatenate([grad_before, next_rows], 0), taps, CONV - 1, -1, row_count
    )
    tap_grads = [
        jnp.sum(grad_before * extended[k : k + row_count], axis=0) for k in range(CONV)
    ]
    offset_grad = jnp.sum(grad_before, axis=0)
    grad_conv_low = jnp.concatenate(
        [grad_conv_in, jnp.pad(grad_raw, ((0, 0), (0, EXTRA - HEADS)))], 1
    ).astype(jnp.bfloat16)
    gate_w_grad = contract_rows(normed, grad_gate_low)
    conv_w_grad = contract_rows(normed, grad_conv_low)
    grad_normed_in = contract_cols(grad_gate_low, gate_w) + contract_cols(grad_conv_low, conv_w)
    grad_input, gain_in_grad = pull_norm(grad_normed_in)
    weight_grads = (gate_w_grad, conv_w_grad, out_grad)
    small_grads = (gain_in_grad, tap_grads, offset_grad, gain_out_grad)
    return (grad_hidden + grad_input, weight_grads, small_grads, (bias_grad, decay_grad, skip_grad))


def on_device(
    inputs,
    cotangent,
    norm_gain,
    proj_weight,
    step_weight,
    conv_weight,
    conv_bias,
    gate_gain,
    out_weight,
    step_bias,
    decay_log,
    skip_scale,
):
    count = lax.axis_size(AXES)
    orders = bit_orders()
    d_own, ch_own, in_own = (norm_gain.shape[1], conv_bias.shape[1], gate_gain.shape[1])
    smalls = jnp.concatenate(
        [
            norm_gain.reshape(-1),
            gate_gain.reshape(-1),
            conv_bias.reshape(-1),
            conv_weight.reshape(-1),
        ]
    )
    smalls = gather_bits(smalls, orders[0]).astype(jnp.float32)
    cut = 0
    rows = []
    for own, number in ((d_own, LAYERS), (in_own, LAYERS), (ch_own, LAYERS), (ch_own, LAYERS * CONV)):
        rows.append([smalls[:, cut + i * own : cut + (i + 1) * own].reshape(-1) for i in range(number)])
        cut += own * number
    gain_rows, gate_rows, bias_rows, tap_rows = rows

    def gather_layer(shards):
        gate_part, conv_part, out_part = shards
        return (
            gather_bits(gate_part, orders[0]).reshape(-1, INNER),
            gather_bits(conv_part, orders[1]).reshape(-1, CHANNELS + EXTRA),
            gather_bits(out_part, orders[2]).reshape(INNER, -1),
        )

    shards = []
    for layer in range(LAYERS):
        shards.append(
            (
                proj_weight[layer, :, :INNER],
                jnp.concatenate(
                    [
                        proj_weight[layer, :, INNER:],
                        jnp.pad(step_weight[layer], ((0, 0), (0, EXTRA - HEADS))),
                    ],
                    1,
                ),
                out_weight[layer],
            )
        )
    gathered = []
    for layer in range(LAYERS):
        if layer > 0:
            shards[layer], _ = lax.optimization_barrier((shards[layer], gathered[layer - 1]))
        gathered.append(gather_layer(shards[layer]))

    hidden = inputs.astype(jnp.float32)
    saved_list, params_list = ([], [])
    for layer in range(LAYERS):
        gate_w, conv_w, out_w = gathered[layer]
        params = (
            gain_rows[layer],
            gate_w,
            conv_w,
            tap_rows[layer * CONV : (layer + 1) * CONV],
            bias_rows[layer],
            gate_rows[layer],
            out_w,
        )
        params_list.append(params)
        head_params = (step_bias[layer], decay_log[layer], skip_scale[layer])
        hidden, kept_values = forward_layer(hidden, params, head_params)
        saved_list.append(kept_values)
    outputs = hidden.astype(jnp.bfloat16)
    grad_hidden = cotangent.astype(jnp.float32)
    summed = [None] * LAYERS
    small_list = [None] * LAYERS
    head_list = [None] * LAYERS
    for layer in reversed(range(LAYERS)):
        head_params = (step_bias[layer], decay_log[layer], skip_scale[layer])
        grad_hidden, weight_grads, small_grads, head_grads = backward_layer(
            grad_hidden, params_list[layer], head_params, saved_list[layer]
        )
        summed[layer] = tuple(
            scatter_bits(
                grad.astype(jnp.bfloat16).reshape(count, -1, grad.shape[1]), order, jnp.bfloat16
            )
            for grad, order in zip(weight_grads, orders)
        )
        gain_in_grad, tap_grads, offset_grad, gain_out_grad = small_grads
        small_list[layer] = jnp.concatenate(
            [line.reshape(count, -1) for line in (gain_in_grad, gain_out_grad, offset_grad, *tap_grads)], 1
        )
        head_list[layer] = jnp.stack(head_grads)
    small_sums = scatter_bits(jnp.stack(small_list, 1), orders[0], jnp.float32)
    head_sums = sum_all(jnp.stack(head_list, 1))
    edge = d_own + in_own
    proj_all = jnp.stack(
        [jnp.concatenate([gate, conv[:, :CHANNELS]], 1) for gate, conv, _ in summed]
    )
    rate_all = jnp.stack([conv[:, CHANNELS : CHANNELS + HEADS] for _, conv, _ in summed])
    out_all = jnp.stack([out for _, _, out in summed])
    return (
        outputs,
        grad_hidden,
        small_sums[:, :d_own],
        proj_all,
        rate_all,
        small_sums[:, edge + ch_own :].reshape(LAYERS, CONV, ch_own),
        small_sums[:, edge : edge + ch_own],
        small_sums[:, d_own:edge],
        out_all,
        head_sums[0],
        head_sums[1],
        head_sums[2],
    )


def solution(mesh):
    in_specs = (
        P(("dp", "ctx"), None),
        P(("dp", "ctx"), None),
        P(None, ("dp", "ctx")),
        P(None, ("dp", "ctx"), None),
        P(None, ("dp", "ctx"), None),
        P(None, None, ("dp", "ctx")),
        P(None, ("dp", "ctx")),
        P(None, ("dp", "ctx")),
        P(None, ("dp", "ctx"), None),
        P(),
        P(),
        P(),
    )
    out_specs = (
        P(("dp", "ctx"), None),
        P(("dp", "ctx"), None),
        P(None, ("dp", "ctx")),
        P(None, ("dp", "ctx"), None),
        P(None, ("dp", "ctx"), None),
        P(None, None, ("dp", "ctx")),
        P(None, ("dp", "ctx")),
        P(None, ("dp", "ctx")),
        P(None, ("dp", "ctx"), None),
        P(),
        P(),
        P(),
    )
    return jax.shard_map(
        on_device, mesh=mesh, in_specs=in_specs, out_specs=out_specs, check_vma=False
    )
```

```python
import jax
import jax.numpy as jnp
from jax import lax
from jax.experimental import pallas as pl
from jax.experimental.pallas import tpu as pltpu
from jax.sharding import PartitionSpec as P

HEADS = 24
HDIM = 64
STATE = 128
CONV = 4
GROUP = 256
LAYERS = 2
INNER = 1536
CHANNELS = INNER + 2 * STATE
EXTRA = 128


EPSILON = 1e-05


def passed_along(block, axis, distance):
    devices = range(lax.axis_size(axis))
    route = [(i - distance, i) for i in devices if i - distance in devices]
    return lax.ppermute(block, axis, route)


AXES = ("dp", "ctx")


def swap_with(block, bit):
    count = lax.axis_size(AXES)
    return lax.ppermute(block, AXES, [(i, i ^ (1 << bit)) for i in range(count)])


def bit_orders():
    ctx_bits = lax.axis_size("ctx").bit_length() - 1
    all_bits = (lax.axis_size(AXES)).bit_length() - 1
    y_bits = list(range(1, ctx_bits))
    x_bits = [ctx_bits]
    z_bits = list(range(ctx_bits + 1, all_bits))
    return ([0] + y_bits + x_bits + z_bits, [0] + x_bits + z_bits + y_bits, [0] + z_bits + y_bits + x_bits)


def side(bit):
    return lax.rem(lax.div(lax.axis_index(AXES), 1 << bit), 2)


def gather_bits(shard, order):
    held, block = [], shard
    for bit in reversed(order):
        other = swap_with(block, bit)
        at = sum(1 for b in held if b > bit)
        upper = side(bit) == 1
        first = jnp.where(upper, other, block)
        second = jnp.where(upper, block, other)
        block = jnp.stack([first, second], at)
        held.append(bit)
    return block.reshape((-1,) + shard.shape)


def scatter_bits(parts, order, kind):
    bits = len(order)
    shape = parts.shape[1:]
    block = parts.reshape((2,) * bits + shape)
    held = list(range(bits - 1, -1, -1))
    for bit in order:
        at = held.index(bit)
        mine = side(bit)
        keep = lax.dynamic_index_in_dim(block, mine, at, keepdims=False)
        give = lax.dynamic_index_in_dim(block, 1 - mine, at, keepdims=False)
        got = swap_with(give, bit)
        block = keep.astype(jnp.float32) + got.astype(jnp.float32)
        held.remove(bit)
        if held:
            block = block.astype(kind)
    return block


def sum_all(block):
    for bit in range(lax.axis_size(AXES).bit_length() - 1):
        block = block + swap_with(block, bit)
    return block


def prefix(decay, state, axis, reverse):
    peers, place = (lax.axis_size(axis), lax.axis_index(axis))
    states = lax.all_gather(state.astype(jnp.bfloat16), axis)
    factors = lax.all_gather(decay.astype(jnp.bfloat16), axis).astype(jnp.float32)
    total = jnp.zeros_like(state)
    for k in range(peers):
        at = peers - 1 - k if reverse else k
        reached = at > place if reverse else at < place
        stepped = total * factors[at][:, None, None] + states[at].astype(jnp.float32)
        total = jnp.where(reached, stepped, total)
    return total


def rms_scale(values, gain):
    return values * lax.rsqrt(jnp.mean(values * values, axis=-1, keepdims=True) + EPSILON) * gain


def gated_norm(values, gate_in, gain):
    return rms_scale(values * jax.nn.silu(gate_in), gain)


def taps_sum(extended, taps, first, step, row_count):
    total = None
    for k in range(CONV):
        start = first + step * k
        term = taps[k][None, :] * extended[start : start + row_count]
        total = term if total is None else total + term
    return total


def rates(step_raw, step_bias, decay_log):
    step_size = jax.nn.softplus(step_raw + step_bias)
    return (-step_size * jnp.exp(decay_log), step_size)


def mm(left, right, dims, exact=False):
    return lax.dot_general(
        left,
        right,
        ((dims[:1], dims[1:]), ((), ())),
        precision=lax.Precision.HIGHEST if exact else None,
        preferred_element_type=jnp.float32,
    )


PAIR = 2 * HDIM
PAIRS = HEADS // 2


def left_half(rows):
    return lax.broadcasted_iota(jnp.int32, (rows, PAIR), 1) < HDIM


def pair_of(ref, j, half):
    return jnp.where(half, ref[:, 2 * j : 2 * j + 1], ref[:, 2 * j + 1 : 2 * j + 2])


def head_sum(j):
    lane = lax.broadcasted_iota(jnp.int32, (PAIR, 128), 0)
    head = lax.broadcasted_iota(jnp.int32, (PAIR, 128), 1)
    return (head == 2 * j + jnp.where(lane < HDIM, 0, 1)).astype(jnp.float32)


def decay_kernel(cum, cum_t, h, causal):
    difference = cum[:, h : h + 1] - cum_t[h : h + 1, :]
    return jnp.exp(jnp.where(causal, difference, -jnp.inf))


def causal_mask(rows):
    return lax.broadcasted_iota(jnp.int32, (rows, rows), 0) >= lax.broadcasted_iota(
        jnp.int32, (rows, rows), 1
    )


def mix_forward(
    values, write, read, cum, cum_t, step_t, state, gate, skip, gain, normed, mixed, inverse, kept
):
    rows = values.shape[0]
    half, causal = (left_half(rows), causal_mask(rows))
    scores = mm(read[...], write[...], (1, 1))
    squares = jnp.zeros((rows, PAIR), jnp.float32)
    for j in range(PAIRS):
        at = slice(j * PAIR, (j + 1) * PAIR)
        pair = values[:, at]
        parts = []
        for h in (2 * j, 2 * j + 1):
            mixing = scores * decay_kernel(cum, cum_t, h, causal) * step_t[h : h + 1, :]
            parts.append(mm(mixing.astype(jnp.bfloat16), pair, (1, 0)))
        carried = mm(read[...], state[at, :].astype(jnp.bfloat16), (1, 1))
        out = (
            jnp.where(half, parts[0], parts[1])
            + jnp.exp(pair_of(cum, j, half)) * carried
            + skip[:, at] * pair.astype(jnp.float32)
        )
        mixed[:, at] = out
        gated = out * jax.nn.silu(gate[:, at])
        kept[:, at] = gated
        squares += gated * gated
    scale = lax.rsqrt(jnp.sum(squares, axis=1, keepdims=True) / INNER + EPSILON)
    inverse[...] = jnp.broadcast_to(scale, (rows, PAIR))
    for j in range(PAIRS):
        at = slice(j * PAIR, (j + 1) * PAIR)
        normed[:, at] = (kept[:, at] * scale * gain[:, at]).astype(jnp.bfloat16)


def gate_backward(
    grad, values, read, cum, state, gate, gain, mixed, inverse,
    grad_y, grad_gate, gain_grad, skip_grad, growth_grad, read_grad, held_grad,
):
    rows = values.shape[0]
    half = left_half(rows)
    scale = inverse[...]
    total = jnp.zeros((rows, PAIR), jnp.float32)
    for j in range(PAIRS):
        at = slice(j * PAIR, (j + 1) * PAIR)
        unit = mixed[:, at] * jax.nn.silu(gate[:, at]) * scale
        product = grad[:, at] * unit
        gain_grad[:, at] = jnp.sum(product, axis=0, keepdims=True)
        total += product * gain[:, at]
    mean = jnp.sum(total, axis=1, keepdims=True) / INNER
    growths = jnp.zeros((rows, 128), jnp.float32)
    reads = jnp.zeros((rows, STATE), jnp.float32)
    for j in range(PAIRS):
        at = slice(j * PAIR, (j + 1) * PAIR)
        gate_now, mixed_now = (gate[:, at], mixed[:, at])
        sig = jax.nn.sigmoid(gate_now)
        silu = gate_now * sig
        direct = scale * (grad[:, at] * gain[:, at] - mixed_now * silu * scale * mean)
        low = (direct * silu).astype(jnp.bfloat16)
        grad_y[:, at] = low
        slope = sig * (1.0 + gate_now * (1.0 - sig))
        grad_gate[:, at] = (direct * mixed_now * slope).astype(jnp.bfloat16)
        wide = low.astype(jnp.float32)
        held = state[at, :].astype(jnp.bfloat16)
        carried = mm(read[...], held, (1, 1))
        growths += mm(wide * carried, head_sum(j), (1, 0), True)
        skip_grad[:, at] = jnp.sum(wide * values[:, at].astype(jnp.float32), axis=0, keepdims=True)
        grad_carried = (jnp.exp(pair_of(cum, j, half)) * wide).astype(jnp.bfloat16)
        reads += mm(grad_carried, held, (1, 0))
        held_grad[at, :] = mm(grad_carried, read[...], (0, 0))
    growth_grad[...] = growths
    read_grad[...] = reads


def mix_backward(
    grad_y, values, write, read, cum, cum_t, step_t, weight, after, skip, read_part,
    grad_values, grad_write, grad_read, row_grad, column_grad, weight_grad,
):
    rows = values.shape[0]
    half, causal = (left_half(rows), causal_mask(rows))
    scores = mm(read[...], write[...], (1, 1))
    score_grad = jnp.zeros((rows, rows), jnp.float32)
    writes = jnp.zeros((rows, STATE), jnp.float32)
    weights = jnp.zeros((rows, 128), jnp.float32)
    for j in range(PAIRS):
        at = slice(j * PAIR, (j + 1) * PAIR)
        pair, upper = (values[:, at], grad_y[:, at])
        wide, upper_wide = (pair.astype(jnp.float32), upper.astype(jnp.float32))
        update = after[at, :].astype(jnp.bfloat16)
        scaled_grad = mm(write[...], update, (1, 1))
        spread = pair_of(weight, j, half)
        writes += mm((wide * spread).astype(jnp.bfloat16), update, (1, 0))
        parts = []
        for i in range(2):
            h = 2 * j + i
            own = jnp.where(half if i == 0 else jnp.logical_not(half), upper_wide, 0.0)
            mixing_grad = mm(own.astype(jnp.bfloat16), pair, (1, 1))
            factor = decay_kernel(cum, cum_t, h, causal)
            stepped = factor * step_t[h : h + 1, :]
            mixing = scores * stepped
            score_grad += mixing_grad * stepped
            row_grad[:, h : h + 1] = jnp.sum(mixing_grad * mixing, axis=1, keepdims=True)
            column_grad[h : h + 1, :] = jnp.sum(
                mixing_grad * (scores * factor), axis=0, keepdims=True
            )
            parts.append(mm(mixing.astype(jnp.bfloat16), upper, (0, 0)))
        grad_values[:, at] = (
            jnp.where(half, parts[0], parts[1]) + skip[:, at] * upper_wide + scaled_grad * spread
        )
        weights += mm(scaled_grad * wide, head_sum(j), (1, 0), True)
    low = score_grad.astype(jnp.bfloat16)
    grad_read[...] = read_part[...] + mm(low, write[...], (1, 0))
    grad_write[...] = writes + mm(low, read[...], (0, 0))
    weight_grad[...] = weights


def on_core(body, outs, scratch=()):
    return pl.pallas_call(
        body,
        out_shape=[jax.ShapeDtypeStruct(shape, kind) for shape, kind in outs],
        scratch_shapes=list(scratch),
        compiler_params=pltpu.CompilerParams(vmem_limit_bytes=28 * 1024 * 1024),
    )


def lower_ones(rows):
    return causal_mask(rows).astype(jnp.float32)


def contract_rows(left_side, right_side):
    return lax.dot_general(
        left_side, right_side, (((0,), (0,)), ((), ())), preferred_element_type=jnp.float32
    )


def contract_cols(left_side, right_side):
    return lax.dot_general(
        left_side, right_side, (((1,), (1,)), ((), ())), preferred_element_type=jnp.float32
    )


def forward_layer(hidden, params, head_params):
    gain_in, gate_w, conv_w, taps, offset, gain_out, out_w = params
    step_bias, decay_log, skip_scale = head_params
    row_count = hidden.shape[0]
    assert row_count == GROUP
    scaled_in, pull_norm = jax.vjp(rms_scale, hidden, gain_in)
    normed = scaled_in.astype(jnp.bfloat16)
    conv_step = jnp.dot(normed, conv_w, preferred_element_type=jnp.float32)
    gate_in = jnp.dot(normed, gate_w, preferred_element_type=jnp.float32)
    conv_in = conv_step[:, :CHANNELS]
    step_raw = conv_step[:, CHANNELS : CHANNELS + HEADS]
    edge_rows = passed_along(conv_in[row_count - (CONV - 1) :], "ctx", 1)
    extended = jnp.concatenate([edge_rows, conv_in], 0)
    before_act = offset + taps_sum(extended, taps, 0, 1, row_count)
    act_gate = jax.nn.sigmoid(before_act)
    act = before_act * act_gate
    act_low = act.astype(jnp.bfloat16)
    values = act_low[:, :INNER]
    write_keys = act_low[:, INNER : INNER + STATE]
    read_keys = act_low[:, INNER + STATE :]
    (decay_rate, step_size), pull_rate = jax.vjp(rates, step_raw, step_bias, decay_log)
    cumulative = mm(lower_ones(row_count), decay_rate, (1, 0), True)
    block_total = cumulative[-1]
    shrink = jnp.exp(block_total[None, :] - cumulative)
    weight = shrink * step_size
    cum_t, step_t = (cumulative.T, step_size.T)
    spread = jnp.broadcast_to(weight[:, :, None], (row_count, HEADS, HDIM)).reshape(row_count, INNER)
    scaled = (values.astype(jnp.float32) * spread).astype(jnp.bfloat16)
    update = contract_rows(scaled, write_keys).reshape(HEADS, HDIM, STATE)
    device_decay = jnp.exp(block_total)
    incoming = prefix(device_decay, update, "ctx", False).reshape(INNER, STATE)
    skip_row = jnp.repeat(skip_scale, HDIM)[None, :]
    wide = (row_count, INNER)
    normed_out, mixed_out, inverse = on_core(
        mix_forward,
        [(wide, jnp.bfloat16), (wide, jnp.float32), ((row_count, PAIR), jnp.float32)],
        [pltpu.VMEM(wide, jnp.float32)],
    )(
        values, write_keys, read_keys, cumulative, cum_t, step_t, incoming, gate_in,
        skip_row, gain_out[None, :],
    )
    branch = jnp.dot(normed_out, out_w, preferred_element_type=jnp.float32)
    kept_values = (
        normed,
        pull_norm,
        extended,
        before_act,
        act_gate,
        pull_rate,
        values,
        write_keys,
        read_keys,
        cumulative,
        cum_t,
        step_t,
        step_size,
        shrink,
        weight,
        device_decay,
        incoming,
        skip_row,
        gate_in,
        mixed_out,
        inverse,
        normed_out,
    )
    return (hidden + branch, kept_values)


def backward_layer(grad_hidden, params, head_params, kept_values):
    gain_in, gate_w, conv_w, taps, offset, gain_out, out_w = params
    skip_scale = head_params[2]
    (
        normed,
        pull_norm,
        extended,
        before_act,
        act_gate,
        pull_rate,
        values,
        write_keys,
        read_keys,
        cumulative,
        cum_t,
        step_t,
        step_size,
        shrink,
        weight,
        device_decay,
        incoming,
        skip_row,
        gate_in,
        mixed_out,
        inverse,
        normed_out,
    ) = kept_values
    row_count = grad_hidden.shape[0]
    grad_branch = grad_hidden.astype(jnp.bfloat16)
    out_grad = contract_rows(normed_out, grad_branch)
    grad_normed = contract_cols(grad_branch, out_w)
    wide, keys = ((row_count, INNER), (row_count, STATE))
    row = (1, INNER)
    grad_y, grad_gate_low, gain_out_grad, skip_grad, growth_grad, read_part, grad_held = on_core(
        gate_backward,
        [
            (wide, jnp.bfloat16), (wide, jnp.bfloat16), (row, jnp.float32), (row, jnp.float32),
            ((row_count, 128), jnp.float32), (keys, jnp.float32), ((INNER, STATE), jnp.float32),
        ],
    )(grad_normed, values, read_keys, cumulative, incoming, gate_in, gain_out[None, :], mixed_out, inverse)
    skip_grad = jnp.sum(skip_grad.reshape(HEADS, HDIM), axis=1)
    outgoing = prefix(device_decay, grad_held.reshape(HEADS, HDIM, STATE), "ctx", True)
    grad_total = device_decay * jnp.sum(
        outgoing * incoming.reshape(HEADS, HDIM, STATE), axis=(1, 2)
    )
    grad_values, grad_write, grad_read, row_grad, column_grad, weight_grad = on_core(
        mix_backward,
        [
            (wide, jnp.float32), (keys, jnp.float32), (keys, jnp.float32),
            ((row_count, HEADS), jnp.float32), ((HEADS, row_count), jnp.float32),
            ((row_count, 128), jnp.float32),
        ],
    )(
        grad_y, values, write_keys, read_keys, cumulative, cum_t, step_t, weight,
        outgoing.reshape(INNER, STATE), skip_row, read_part,
    )
    growth_grad, weight_grad = (growth_grad[:, :HEADS], weight_grad[:, :HEADS])
    column_grad = column_grad.T
    through_weight = weight * weight_grad
    grad_cum = (
        row_grad - step_size * column_grad + jnp.exp(cumulative) * growth_grad - through_weight
    )
    grad_total = grad_total + jnp.sum(through_weight, axis=0)
    grad_rate = mm(lower_ones(row_count), grad_cum, (0, 0), True) + grad_total
    grad_step = column_grad + shrink * weight_grad
    grad_raw, bias_grad, decay_grad = pull_rate((grad_rate, grad_step))
    grad_act = jnp.concatenate([grad_values, grad_write, grad_read], 1)
    grad_before = grad_act * (act_gate * (1.0 + before_act * (1.0 - act_gate)))
    next_rows = passed_along(grad_before[: CONV - 1], "ctx", -1)
    grad_conv_in = taps_sum(
        jnp.concatenate([grad_before, next_rows], 0), taps, CONV - 1, -1, row_count
    )
    tap_grads = [
        jnp.sum(grad_before * extended[k : k + row_count], axis=0) for k in range(CONV)
    ]
    offset_grad = jnp.sum(grad_before, axis=0)
    grad_conv_low = jnp.concatenate(
        [grad_conv_in, jnp.pad(grad_raw, ((0, 0), (0, EXTRA - HEADS)))], 1
    ).astype(jnp.bfloat16)
    gate_w_grad = contract_rows(normed, grad_gate_low)
    conv_w_grad = contract_rows(normed, grad_conv_low)
    grad_normed_in = contract_cols(grad_gate_low, gate_w) + contract_cols(grad_conv_low, conv_w)
    grad_input, gain_in_grad = pull_norm(grad_normed_in)
    weight_grads = (gate_w_grad, conv_w_grad, out_grad)
    small_grads = (gain_in_grad, tap_grads, offset_grad, gain_out_grad)
    return (grad_hidden + grad_input, weight_grads, small_grads, (bias_grad, decay_grad, skip_grad))


def on_device(
    inputs,
    cotangent,
    norm_gain,
    proj_weight,
    step_weight,
    conv_weight,
    conv_bias,
    gate_gain,
    out_weight,
    step_bias,
    decay_log,
    skip_scale,
):
    count = lax.axis_size(AXES)
    orders = bit_orders()
    d_own, ch_own, in_own = (norm_gain.shape[1], conv_bias.shape[1], gate_gain.shape[1])
    smalls = jnp.concatenate(
        [
            norm_gain.reshape(-1),
            gate_gain.reshape(-1),
            conv_bias.reshape(-1),
            conv_weight.reshape(-1),
        ]
    )
    smalls = gather_bits(smalls, orders[0]).astype(jnp.float32)
    cut = 0
    rows = []
    for own, number in ((d_own, LAYERS), (in_own, LAYERS), (ch_own, LAYERS), (ch_own, LAYERS * CONV)):
        rows.append([smalls[:, cut + i * own : cut + (i + 1) * own].reshape(-1) for i in range(number)])
        cut += own * number
    gain_rows, gate_rows, bias_rows, tap_rows = rows

    def gather_layer(shards):
        gate_part, conv_part, out_part = shards
        return (
            gather_bits(gate_part, orders[0]).reshape(-1, INNER),
            gather_bits(conv_part, orders[1]).reshape(-1, CHANNELS + EXTRA),
            gather_bits(out_part, orders[2]).reshape(INNER, -1),
        )

    shards = []
    for layer in range(LAYERS):
        shards.append(
            (
                proj_weight[layer, :, :INNER],
                jnp.concatenate(
                    [
                        proj_weight[layer, :, INNER:],
                        jnp.pad(step_weight[layer], ((0, 0), (0, EXTRA - HEADS))),
                    ],
                    1,
                ),
                out_weight[layer],
            )
        )
    gathered = []
    for layer in range(LAYERS):
        if layer > 0:
            shards[layer], _ = lax.optimization_barrier((shards[layer], gathered[layer - 1]))
        gathered.append(gather_layer(shards[layer]))

    hidden = inputs.astype(jnp.float32)
    saved_list, params_list = ([], [])
    for layer in range(LAYERS):
        gate_w, conv_w, out_w = gathered[layer]
        params = (
            gain_rows[layer],
            gate_w,
            conv_w,
            tap_rows[layer * CONV : (layer + 1) * CONV],
            bias_rows[layer],
            gate_rows[layer],
            out_w,
        )
        params_list.append(params)
        head_params = (step_bias[layer], decay_log[layer], skip_scale[layer])
        hidden, kept_values = forward_layer(hidden, params, head_params)
        saved_list.append(kept_values)
    outputs = hidden.astype(jnp.bfloat16)
    grad_hidden = cotangent.astype(jnp.float32)
    summed = [None] * LAYERS
    small_list = [None] * LAYERS
    head_list = [None] * LAYERS
    for layer in reversed(range(LAYERS)):
        head_params = (step_bias[layer], decay_log[layer], skip_scale[layer])
        grad_hidden, weight_grads, small_grads, head_grads = backward_layer(
            grad_hidden, params_list[layer], head_params, saved_list[layer]
        )
        summed[layer] = weight_grads
        gain_in_grad, tap_grads, offset_grad, gain_out_grad = small_grads
        small_list[layer] = jnp.concatenate(
            [line.reshape(count, -1) for line in (gain_in_grad, gain_out_grad, offset_grad, *tap_grads)], 1
        )
        head_list[layer] = jnp.stack(head_grads)
    small_sums = scatter_bits(jnp.stack(small_list, 1), orders[0], jnp.float32)
    head_sums = sum_all(jnp.stack(head_list, 1))
    edge = d_own + in_own
    gate_all, conv_all, out_all = (
        scatter_bits(
            jnp.stack(
                [grad.astype(jnp.bfloat16).reshape(count, -1, grad.shape[1]) for grad in grads], 1
            ),
            order,
            jnp.bfloat16,
        )
        for grads, order in zip(zip(*summed), orders)
    )
    proj_all = jnp.concatenate([gate_all, conv_all[:, :, :CHANNELS]], 2)
    rate_all = conv_all[:, :, CHANNELS : CHANNELS + HEADS]
    return (
        outputs,
        grad_hidden,
        small_sums[:, :d_own],
        proj_all,
        rate_all,
        small_sums[:, edge + ch_own :].reshape(LAYERS, CONV, ch_own),
        small_sums[:, edge : edge + ch_own],
        small_sums[:, d_own:edge],
        out_all,
        head_sums[0],
        head_sums[1],
        head_sums[2],
    )


def solution(mesh):
    in_specs = (
        P(("dp", "ctx"), None),
        P(("dp", "ctx"), None),
        P(None, ("dp", "ctx")),
        P(None, ("dp", "ctx"), None),
        P(None, ("dp", "ctx"), None),
        P(None, None, ("dp", "ctx")),
        P(None, ("dp", "ctx")),
        P(None, ("dp", "ctx")),
        P(None, ("dp", "ctx"), None),
        P(),
        P(),
        P(),
    )
    out_specs = (
        P(("dp", "ctx"), None),
        P(("dp", "ctx"), None),
        P(None, ("dp", "ctx")),
        P(None, ("dp", "ctx"), None),
        P(None, ("dp", "ctx"), None),
        P(None, None, ("dp", "ctx")),
        P(None, ("dp", "ctx")),
        P(None, ("dp", "ctx")),
        P(None, ("dp", "ctx"), None),
        P(),
        P(),
        P(),
    )
    return jax.shard_map(
        on_device, mesh=mesh, in_specs=in_specs, out_specs=out_specs, check_vma=False
    )
```
